256 devices in a mesh: frame: 16 (over x, z_hi, core), patch: 16 (over y, z_lo).
Axes of the slice: x: 4, y: 4, z: 8 (z_hi: 2, z_lo: 4; z = z_hi * 4 + z_lo), core: 2. Of those that a mesh axis runs over, the one named last changes fastest.
Arguments:
- latent: bfloat16 [32, 2048, 1536], P('frame', 'patch'), may hold values from -6 to 6
- timesteps: int32 [3], replicated, may hold values from 1 to 999
- w_qkv: bfloat16 [1536, 2304], replicated, may hold values from -2.5 to 2.5
- w_out: bfloat16 [768, 1536], replicated, may hold values from -0.21875 to 0.21875
- w_time: bfloat16 [256, 4608], replicated, may hold values from -0.75 to 0.75
- stale_kv: bfloat16 [32, 2048, 1536], P('frame', 'patch'), may hold values from -9 to 9
Outputs:
- latent_out: bfloat16 [32, 2048, 1536], P('frame', 'patch')
- velocity: bfloat16 [32, 2048, 1536], P('frame', 'patch')
- next_kv: bfloat16 [32, 2048, 1536], P('frame', 'patch')
The draws below stay inside these ranges and needn't reach their ends.
All inputs are finite; a program needn't handle non-finite values.
Results may differ from the reference program's by a relative error of at most 0.028.
Values may be sent and summed in bfloat16 or wider, within the bound.
A program may use at most 128 MiB of HBM per device.

```python
import math
import jax
import jax.numpy as jnp
from jax import lax

MODEL_WIDTH = 1536
HEAD_DIM = 128
FREQ = 256
SHEADS = 3
THEADS = 3
STEPS = 2
FR_DEV = 2
SP_DEV = 128
FRAMES = 32
SPATIAL = 2048


def draw_w_qkv(key, part):
    key = jax.random.fold_in(key, 11)
    query_random_seed, key_random_seed, value_random_seed = jax.random.split(key, 3)
    model_width = (SHEADS + THEADS) * HEAD_DIM
    swidth = SHEADS * HEAD_DIM
    value_deviation = 1.5 / math.sqrt(MODEL_WIDTH)
    queries = jnp.clip(jax.random.normal(query_random_seed, (MODEL_WIDTH, model_width), jnp.float32), -6.0, 6.0) * value_deviation
    keys = jnp.clip(jax.random.normal(key_random_seed, (MODEL_WIDTH, model_width), jnp.float32), -6.0, 6.0) * value_deviation
    value_rows = jnp.clip(jax.random.normal(value_random_seed, (MODEL_WIDTH, model_width), jnp.float32), -6.0, 6.0) * value_deviation
    whole = jnp.concatenate([queries, keys[:, :swidth], value_rows[:, :swidth], keys[:, swidth:], value_rows[:, swidth:]], axis=1)
    whole = jnp.clip(whole, -2.5, 2.5)
    return whole.astype(jnp.bfloat16)


def block_scale(rng, extent, cuts, low, largest):
    def one(axis_at, parts):
        heights = jax.random.uniform(jax.random.fold_in(jax.random.fold_in(rng, 6), axis_at), (parts,), jnp.float32, low / len(cuts), largest / len(cuts))
        return jnp.repeat(jnp.exp(heights), extent[axis_at] // parts).reshape((-1,) + (1,) * (len(extent) - axis_at - 1))

    loudness = one(*cuts[0])
    for cut in cuts[1:]:
        loudness = loudness * one(*cut)
    return loudness


def gaussian(own_key, extent, scale, bound, shards=(), held_as=jnp.bfloat16):
    loudness = block_scale(own_key, extent, shards, -0.22, 0.18) if shards else 1.0
    result = jax.random.normal(own_key, extent, jnp.float32) * scale * loudness
    return jnp.minimum(jnp.maximum(result, -bound), bound).astype(held_as)


def setup_inputs(seed: int = 0) -> dict:
    key_list = jax.random.split(jax.random.key(seed), 7)
    return {
        "latent": gaussian(key_list[0], (FRAMES, SPATIAL, MODEL_WIDTH), 1.0, 6.0, ((0, 16), (1, 16))),
        "timesteps": jax.random.randint(key_list[1], (STEPS + 1,), 1, 1000).astype(jnp.int32),
        "w_qkv": draw_w_qkv(jax.random.fold_in(key_list[6], 71), 0),
        "w_out": gaussian(key_list[3], ((SHEADS + THEADS) * HEAD_DIM, MODEL_WIDTH), ((SHEADS + THEADS) * HEAD_DIM) ** -0.5, 0.21875),
        "w_time": gaussian(key_list[4], (FREQ, 3 * MODEL_WIDTH), (FREQ // 4) ** -0.5, 0.75),
        "stale_kv": gaussian(key_list[5], (FRAMES, SPATIAL, 2 * (SHEADS + THEADS) * HEAD_DIM), 1.5, 9.0, ((0, 16), (1, 16))),
    }


def sigma_level(index):
    unit = index.astype(jnp.float32) / 1000.0
    return 5.0 * unit / (1.0 + 4.0 * unit)

def modulation(index, w_time):
    level = sigma_level(index) * 1000.0
    half = FREQ // 2
    freqs = jnp.exp(-math.log(10000.0) * jnp.arange(half, dtype=jnp.float32) / half)
    angles = level * freqs
    embed = jnp.concatenate([jnp.cos(angles), jnp.sin(angles)])
    mods = jnp.dot(jax.nn.silu(embed)[None, :], w_time.astype(jnp.float32), precision=lax.Precision.HIGHEST)[0]
    return (mods[:MODEL_WIDTH], mods[MODEL_WIDTH:2 * MODEL_WIDTH], mods[2 * MODEL_WIDTH:])

def normalize(latent):
    value_rows = latent.astype(jnp.float32)
    center = lax.optimization_barrier(jnp.mean(value_rows, axis=-1, keepdims=True))
    value_deviation = lax.optimization_barrier(jnp.mean((value_rows - center) ** 2, axis=-1, keepdims=True))
    return (value_rows - center) / jnp.sqrt(value_deviation + 1e-06)

def softmax_rows(scores):
    top = lax.optimization_barrier(jnp.max(scores, axis=-1, keepdims=True))
    expo = jnp.exp(scores - top)
    return (expo / lax.optimization_barrier(jnp.sum(expo, axis=-1, keepdims=True))).astype(jnp.bfloat16)

def reference(latent, timesteps, w_qkv, w_out, w_time, stale_kv):
    swidth = SHEADS * HEAD_DIM
    twidth = THEADS * HEAD_DIM
    qwidth = swidth + twidth
    factor = 1.0 / math.sqrt(HEAD_DIM)
    current = latent
    previous = stale_kv
    sblock = jnp.arange(SPATIAL) // SP_DEV
    ssame = sblock[:, None] == sblock[None, :]
    fblock = jnp.arange(FRAMES) // FR_DEV
    fsame = fblock[:, None] == fblock[None, :]
    for step in range(STEPS):
        shift, scale, gate = modulation(timesteps[step], w_time)
        dsig = sigma_level(timesteps[step + 1]) - sigma_level(timesteps[step])
        hidden = (normalize(current) * (1.0 + scale) + shift).astype(jnp.bfloat16)
        proj = jnp.dot(hidden.reshape(-1, MODEL_WIDTH), w_qkv, preferred_element_type=jnp.float32).astype(jnp.bfloat16)
        proj = proj.reshape(FRAMES, SPATIAL, -1)
        query = proj[..., :qwidth]
        fresh = proj[..., qwidth:]

        def spatial_frame(frame):
            qf = lax.dynamic_index_in_dim(query, frame, 0, False)[:, :swidth].reshape(SPATIAL, SHEADS, HEAD_DIM).astype(jnp.float32)
            nf = lax.dynamic_index_in_dim(fresh, frame, 0, False)
            of = lax.dynamic_index_in_dim(previous, frame, 0, False)
            kf = nf[:, :swidth].reshape(SPATIAL, SHEADS, HEAD_DIM).astype(jnp.float32)
            vf = nf[:, swidth:2 * swidth].reshape(SPATIAL, SHEADS, HEAD_DIM).astype(jnp.float32)
            ko = of[:, :swidth].reshape(SPATIAL, SHEADS, HEAD_DIM).astype(jnp.float32)
            vo = of[:, swidth:2 * swidth].reshape(SPATIAL, SHEADS, HEAD_DIM).astype(jnp.float32)
            mask = ssame[None, :, :]
            scores = jnp.where(mask, jnp.einsum('qhd,khd->hqk', qf, kf), jnp.einsum('qhd,khd->hqk', qf, ko)) * factor
            weights = softmax_rows(scores)
            zero = jnp.zeros_like(weights)
            part_new = jnp.einsum('hqk,khd->qhd', jnp.where(mask, weights, zero).astype(jnp.float32), vf)
            part_old = jnp.einsum('hqk,khd->qhd', jnp.where(mask, zero, weights).astype(jnp.float32), vo)
            return (part_new + part_old).reshape(SPATIAL, swidth)
        spatial_out = lax.map(spatial_frame, jnp.arange(FRAMES, dtype=jnp.int32))
        qt = query[..., swidth:].reshape(FRAMES, SPATIAL, THEADS, HEAD_DIM).astype(jnp.float32)
        kt = fresh[..., 2 * swidth:2 * swidth + twidth].reshape(FRAMES, SPATIAL, THEADS, HEAD_DIM).astype(jnp.float32)
        vt = fresh[..., 2 * swidth + twidth:].reshape(FRAMES, SPATIAL, THEADS, HEAD_DIM).astype(jnp.float32)
        kto = previous[..., 2 * swidth:2 * swidth + twidth].reshape(FRAMES, SPATIAL, THEADS, HEAD_DIM).astype(jnp.float32)
        vto = previous[..., 2 * swidth + twidth:].reshape(FRAMES, SPATIAL, THEADS, HEAD_DIM).astype(jnp.float32)
        tmask = fsame[None, None, :, :]
        tscores = jnp.where(tmask, jnp.einsum('qphd,kphd->phqk', qt, kt), jnp.einsum('qphd,kphd->phqk', qt, kto)) * factor
        tweights = softmax_rows(tscores)
        tzero = jnp.zeros_like(tweights)
        tnew = jnp.einsum('phqk,kphd->qphd', jnp.where(tmask, tweights, tzero).astype(jnp.float32), vt)
        told = jnp.einsum('phqk,kphd->qphd', jnp.where(tmask, tzero, tweights).astype(jnp.float32), vto)
        temporal_out = (tnew + told).reshape(FRAMES, SPATIAL, twidth)
        attended = jnp.concatenate([spatial_out, temporal_out], axis=-1).astype(jnp.bfloat16)
        branch = jnp.dot(attended.reshape(-1, qwidth), w_out, preferred_element_type=jnp.float32).reshape(FRAMES, SPATIAL, MODEL_WIDTH)
        vel = gate * branch
        current = (current.astype(jnp.float32) + dsig * vel).astype(jnp.bfloat16)
        previous = fresh
    return (current, vel.astype(jnp.bfloat16), previous)
```

```python
import functools
import math

import jax
import jax.numpy as jnp
from jax import lax
from jax.experimental import pallas as pl
from jax.experimental.pallas import tpu as pltpu
from jax.sharding import PartitionSpec as P

MESH = pl.DeviceIdType.MESH
D = 128
SH = 3
TH = 3
WIDTH = 1536
QW = (SH + TH) * D
ROWS = 256
FREQ = 256
STEPS = 2
NEG = -1e30
LOG2 = math.log2(math.e) / math.sqrt(D)
F32 = jnp.float32
BF16 = jnp.bfloat16


def dot_t(a, b):
    return lax.dot_general(a, b, (((1,), (1,)), ((), ())), preferred_element_type=F32)


def iota(shape, dim):
    return lax.broadcasted_iota(jnp.int32, shape, dim)


def split3(value):
    hi = value.astype(BF16).astype(F32)
    mid = (value - hi).astype(BF16).astype(F32)
    return hi, mid, value - hi - mid


def col_to_row(col):
    eye = iota((D, D), 0) == iota((D, D), 1)
    return jnp.sum(jnp.where(eye, col, 0.0), axis=0, keepdims=True)


def sigma_of(index):
    unit = index.astype(F32) / 1000.0
    return 5.0 * unit / (1.0 + 4.0 * unit)


def kernel(
    ts_ref, lat_ref, stale_ref, wqkv_ref, wout_ref, wtime_ref,
    xo_ref, vo_ref, kvo_ref,
    x_v, h_v, vel_v, wqkv_v, wout_v, wtime_v, mods_v,
    qloc, kvloc, kvs, kvt, qs, qt, oss, osr, ots, otr,
    s_v, ol_s, ll_s, ol_t, ll_t, att,
    load_sem, stale_sem, out_sem, kvo_sem,
    ks_s, ks_r, kt_s, kt_r, qs_s, qs_r, qt_s, qt_r, os_s, os_r, ot_s, ot_r,
):
    fi = lax.axis_index("frame")
    pi = lax.axis_index("patch")
    core = lax.rem(fi, 2)
    zh = lax.rem(fi // 2, 2)
    own = (fi // 4) * 2 + core
    half = lax.rem(pi, 4) // 2
    src = (pi // 4) * 2 + lax.rem(pi, 2)
    role = lax.rem(src + 4 * core, 8)

    def patch_at(place, of_half):
        return (place // 2) * 4 + 2 * of_half + lax.rem(place, 2)

    def place_of(pair):
        return lax.rem(pair + 8 - 4 * core, 8)

    def frame_at(owner, group):
        return (owner // 2) * 4 + group * 2 + lax.rem(owner, 2)

    def push(source, target, send, recv, device, is_self):
        @pl.when(is_self)
        def _():
            pltpu.make_async_copy(source, target, recv).start()

        @pl.when(jnp.logical_not(is_self))
        def _():
            pltpu.make_async_remote_copy(
                src_ref=source, dst_ref=target, send_sem=send, recv_sem=recv,
                device_id=device, device_id_type=MESH,
            ).start()

    def take(ref, sem):
        pltpu.make_async_copy(ref, ref, sem).wait()

    def loop(count, body):
        def step(index, carry):
            body(index)
            return carry
        lax.fori_loop(0, count, step, 0)

    def load_stale(block):
        return pltpu.make_async_copy(
            stale_ref.at[:, :, pl.ds(pl.multiple_of(block * D, D), D)],
            kvloc.at[0, block // 3, lax.rem(block, 3)], stale_sem.at[block])

    loop(12, lambda b: load_stale(b).start())
    loads = [
        pltpu.make_async_copy(a, b, load_sem.at[n])
        for n, (a, b) in enumerate(
            [(lat_ref, x_v), (wtime_ref, wtime_v), (wqkv_ref, wqkv_v), (wout_ref, wout_v)])
    ]
    for one in loads:
        one.start()

    barrier = pltpu.get_barrier_semaphore()

    def greet(k):
        pl.semaphore_signal(
            barrier, inc=1, device_id=(fi, lax.rem(pi + k + 1, 16)), device_id_type=MESH)
        pl.semaphore_signal(
            barrier, inc=1, device_id=(lax.rem(fi + k + 1, 16), pi), device_id_type=MESH)

    loop(15, greet)
    loop(12, lambda b: load_stale(b).wait())
    pl.semaphore_wait(barrier, 30)

    def send_kv(k):
        def spatial(n):
            to_half = n // 6
            pair = lax.rem(n, 6)
            frame, head = pair // 3, lax.rem(pair, 3)
            device = patch_at(place_of(pair), to_half)
            slot = src + 8 * jnp.where(to_half == half, 0, 1)
            push(kvloc.at[k, 0:2, head, frame], kvs.at[k, :, slot], ks_s.at[k, n], ks_r.at[k, slot],
                 (fi, device), device == pi)

        def temporal(n):
            group, owner = n // 8, lax.rem(n, 8)
            device = frame_at(owner, group)
            slot = own + 8 * jnp.where(group == zh, 0, 1)
            rows = pl.ds(pl.multiple_of(owner * 16, 16), 16)
            push(kvloc.at[k, 2:4, :, :, rows], kvt.at[k, :, :, slot], kt_s.at[k, n], kt_r.at[k, slot],
                 (device, pi), device == fi)

        loop(12, spatial)
        loop(16, temporal)

    send_kv(0)

    loads[1].wait()
    lane = iota((16, D), 1).astype(F32)
    row = iota((16, D), 0)
    level = jnp.where(
        row < 3, sigma_of(jnp.full((16, D), ts_ref[0], jnp.int32)),
        sigma_of(jnp.full((16, D), ts_ref[1], jnp.int32))) * 1000.0
    angles = level * jnp.exp(-math.log(10000.0) * lane / D)
    part = lax.rem(row, 3)

    def embed(value):
        value = value / (1.0 + jnp.exp(-value))
        hi, mid, low = split3(value)
        return jnp.where(part == 0, hi, jnp.where(part == 1, mid, low)).astype(BF16)

    emb = jnp.concatenate([embed(jnp.cos(angles)), embed(jnp.sin(angles))], axis=1)
    for n in range(0, 3 * WIDTH, 512):
        cols = slice(n, n + 512)
        parts = jnp.dot(emb, wtime_v[:, cols], preferred_element_type=F32)
        for k in range(STEPS):
            mods_v[k : k + 1, cols] = jnp.sum(parts[3 * k : 3 * k + 3], axis=0, keepdims=True)

    loads[0].wait()

    for k in range(STEPS):
        def norm(n):
            rows = pl.ds(pl.multiple_of(n * 32, 32), 32)
            value = x_v[rows, :].astype(F32)
            center = jnp.mean(value, axis=-1, keepdims=True)
            value = value - center
            spread = jnp.mean(value * value, axis=-1, keepdims=True)
            value = value * lax.rsqrt(spread + 1e-06)
            h_v[rows, :] = (
                value * (1.0 + mods_v[k : k + 1, WIDTH : 2 * WIDTH]) + mods_v[k : k + 1, :WIDTH]
            ).astype(BF16)

        loop(ROWS // 32, norm)
        if k == 0:
            loads[2].wait()

        def project(n):
            cols = pl.ds(pl.multiple_of(n * 256, 256), 256)
            return jnp.dot(h_v[...], wqkv_v[:, cols], preferred_element_type=F32).astype(BF16)

        def query(n):
            out = project(n)
            for part_n in range(2):
                qloc[2 * n + part_n] = out[:, part_n * D : (part_n + 1) * D].reshape(2, D, D)

        if k > 0:
            def sent_q(n):
                @pl.when((n < 6) & (n != role))
                def _():
                    take(qs.at[k - 1, 0], qs_s.at[k - 1, n])

                @pl.when(n != own)
                def _():
                    take(qt.at[k - 1, :, 0], qt_s.at[k - 1, n])

            loop(8, sent_q)
        loop(3, query)

        def send_q(pair):
            place = place_of(pair)
            frame, head = pair // 3, lax.rem(pair, 3)
            push(qloc.at[head, frame], qs.at[k, src], qs_s.at[k, pair], qs_r.at[k, src],
                 (fi, patch_at(place, half)), place == src)

        def send_qt(owner):
            rows = pl.ds(pl.multiple_of(owner * 16, 16), 16)
            push(qloc.at[3:6, :, rows], qt.at[k, :, own], qt_s.at[k, owner], qt_r.at[k, own],
                 (frame_at(owner, zh), pi), owner == own)

        loop(6, send_q)
        loop(8, send_qt)

        def fresh(n):
            out = project(n + 3)
            for part_n in range(2):
                block = 2 * n + part_n
                kvloc[k + 1, block // 3, lax.rem(block, 3)] = out[:, part_n * D : (part_n + 1) * D].reshape(2, D, D)

        loop(6, fresh)

        def store_kv(block):
            return pltpu.make_async_copy(
                kvloc.at[STEPS, block // 3, lax.rem(block, 3)],
                kvo_ref.at[:, :, pl.ds(pl.multiple_of(block * D, D), D)], kvo_sem.at[block])

        if k + 1 < STEPS:
            send_kv(k + 1)
        else:
            loop(12, lambda b: store_kv(b).start())

        def local_spatial(pair):
            frame, head = pair // 3, lax.rem(pair, 3)
            scores = dot_t(qloc[head, frame], kvloc[k + 1, 0, head, frame]) * LOG2
            top = jnp.max(scores, axis=-1, keepdims=True)
            expo = jnp.exp2(scores - top)
            total = jnp.sum(expo, axis=-1, keepdims=True)
            out = jnp.dot(expo.astype(BF16), kvloc[k + 1, 1, head, frame], preferred_element_type=F32)
            ol_s[pair] = out / total
            ll_s[pair] = top + jnp.log2(total)

        loop(6, local_spatial)

        def local_temporal(head):
            for frame in range(2):
                q = qloc[3 + head, frame].astype(F32)
                s0, s1 = [
                    jnp.sum(q * kvloc[k + 1, 2, head, f].astype(F32), axis=-1, keepdims=True) * LOG2
                    for f in range(2)
                ]
                top = jnp.maximum(s0, s1)
                e0, e1 = jnp.exp2(s0 - top), jnp.exp2(s1 - top)
                total = e0 + e1
                out = e0 * kvloc[k + 1, 3, head, 0].astype(F32) + e1 * kvloc[k + 1, 3, head, 1].astype(F32)
                ol_t[head, frame] = out / total
                ll_t[head, frame] = top + jnp.log2(total)

        loop(3, local_temporal)

        @pl.when(role < 6)
        def _():
            def arrived(n):
                take(kvs.at[k, :, n], ks_r.at[k, n])

            def arrived_q(n):
                take(qs.at[k, n], qs_r.at[k, n])

            loop(8, arrived_q)
            loop(16, arrived)

            def attend(n):
                q = qs[k, pl.ds(2 * n, 2)].reshape(2 * D, D)
                s_v[...] = dot_t(q, kvs[k, 0].reshape(16 * D, D))
                base = pl.multiple_of(n * 2 * D, 2 * D)
                s_v[0:D, pl.ds(base, D)] = jnp.full((D, D), NEG, F32)
                s_v[D : 2 * D, pl.ds(pl.multiple_of(base + D, D), D)] = jnp.full((D, D), NEG, F32)
                scores = s_v[...]
                top = jnp.max(scores, axis=-1, keepdims=True)
                expo = jnp.exp2((scores - top) * LOG2)
                total = jnp.sum(expo, axis=-1, keepdims=True)
                out = jnp.dot(expo.astype(BF16), kvs[k, 1].reshape(16 * D, D), preferred_element_type=F32)
                out = (out / total).astype(BF16)
                lse = top * LOG2 + jnp.log2(total)
                for part_n in range(2):
                    place = 2 * n + part_n
                    oss[k, place, 0:D] = out[part_n * D : (part_n + 1) * D]
                    hi, mid, low = split3(col_to_row(lse[part_n * D : (part_n + 1) * D]))
                    tile = iota((16, D), 0)
                    oss[k, place, D : D + 16] = jnp.where(
                        tile == 0, hi, jnp.where(tile == 1, mid, jnp.where(tile == 2, low, 0.0))).astype(BF16)
                    push(oss.at[k, place], osr.at[k, role], os_s.at[k, place], os_r.at[k, role],
                         (fi, patch_at(place, half)), place == src)

            loop(4, attend)

        loop(8, lambda n: take(qt.at[k, :, n], qt_r.at[k, n]))
        loop(16, lambda n: take(kvt.at[k, :, :, n], kt_r.at[k, n]))
        rows_i, cols_i = iota((ROWS, 2 * ROWS), 0), iota((ROWS, 2 * ROWS), 1)
        seen = (lax.rem(rows_i, 16) == lax.rem(cols_i, 16)) & (rows_i // 32 != cols_i // 32)
        tile = iota((16, D), 0)
        stats = [jnp.zeros((16, D), F32), jnp.zeros((16, D), F32)]
        for head in range(TH):
            scores = dot_t(qt[k, head].reshape(ROWS, D), kvt[k, 0, head].reshape(2 * ROWS, D))
            scores = jnp.where(seen, scores, NEG)
            top = jnp.max(scores, axis=-1, keepdims=True)
            expo = jnp.exp2((scores - top) * LOG2)
            total = jnp.sum(expo, axis=-1, keepdims=True)
            out = jnp.dot(
                expo.astype(BF16), kvt[k, 1, head].reshape(2 * ROWS, D), preferred_element_type=F32)
            out = (out / total).astype(BF16)
            lse = top * LOG2 + jnp.log2(total)
            ots[k, :, head * 32 : head * 32 + 32] = out.reshape(8, 32, D)
            for chunk in range(2):
                parts = split3(col_to_row(lse[chunk * D : (chunk + 1) * D]))
                for n, value in enumerate(parts):
                    stats[chunk] = jnp.where(tile == 3 * head + n, value, stats[chunk])
        for place in range(8):
            ots[k, place, 96:112] = stats[place // 4].astype(BF16)

        def send_ot(place):
            push(ots.at[k, place], otr.at[k, own], ot_s.at[k, place], ot_r.at[k, own],
                 (frame_at(place, zh), pi), place == own)

        loop(8, send_ot)

        def merge(mine, mine_lse, other, other_lse):
            weight = 1.0 / (1.0 + jnp.exp2(mine_lse - other_lse))
            return (mine + weight * (other.astype(F32) - mine)).astype(BF16)

        for pair in range(6):
            take(osr.at[k, pair], os_r.at[k, pair])
            frame, head = pair // 3, pair % 3
            lse = jnp.sum(osr[k, pair, D : D + 16].astype(F32), axis=0, keepdims=True)
            eye = iota((D, D), 0) == iota((D, D), 1)
            lse = jnp.sum(jnp.where(eye, lse, 0.0), axis=1, keepdims=True)
            att[frame * D : (frame + 1) * D, head * D : (head + 1) * D] = merge(
                ol_s[pair], ll_s[pair], osr[k, pair, 0:D], lse)

        loop(8, lambda n: take(otr.at[k, n], ot_r.at[k, n]))
        pick = iota((32, D), 1) == iota((32, D), 0) + 32 * lax.rem(own, 4)

        def merge_t(owner):
            stat = otr[k, owner, 96:112].astype(F32)
            for head in range(TH):
                lse = jnp.sum(stat[3 * head : 3 * head + 3], axis=0, keepdims=True)
                lse = jnp.sum(jnp.where(pick, lse, 0.0), axis=1, keepdims=True)
                for frame in range(2):
                    rows = pl.ds(pl.multiple_of(owner * 16, 16), 16)
                    att[
                        pl.ds(pl.multiple_of(frame * D + owner * 16, 16), 16),
                        (SH + head) * D : (SH + head + 1) * D,
                    ] = merge(
                        ol_t[head, frame, rows], ll_t[head, frame, rows],
                        otr[k, owner, head * 32 + frame * 16 : head * 32 + frame * 16 + 16],
                        lse[frame * 16 : frame * 16 + 16])

        loop(8, merge_t)

        if k == 0:
            loads[3].wait()
        dsig = (sigma_of(jnp.full((1, 256), ts_ref[k + 1], jnp.int32))
                - sigma_of(jnp.full((1, 256), ts_ref[k], jnp.int32)))

        def stores(n):
            cols = pl.ds(pl.multiple_of(n * 256, 256), 256)
            return [
                pltpu.make_async_copy(x_v.at[:, cols], xo_ref.at[:, cols], out_sem.at[0, n]),
                pltpu.make_async_copy(vel_v.at[:, cols], vo_ref.at[:, cols], out_sem.at[1, n]),
            ]

        def update(n):
            cols = pl.ds(pl.multiple_of(n * 256, 256), 256)
            branch = jnp.dot(att[...], wout_v[:, cols], preferred_element_type=F32)
            vel = mods_v[k : k + 1, pl.ds(pl.multiple_of(2 * WIDTH + n * 256, 256), 256)] * branch
            x_v[:, cols] = (x_v[:, cols].astype(F32) + dsig * vel).astype(BF16)
            if k + 1 == STEPS:
                vel_v[:, cols] = vel.astype(BF16)
                for one in stores(n):
                    one.start()

        loop(WIDTH // 256, update)

    def drained(n):
        for one in stores(n):
            one.wait()

    loop(WIDTH // 256, drained)
    loop(12, lambda b: store_kv(b).wait())
    for k in range(STEPS):
        def sent_ks(n):
            @pl.when(jnp.logical_not((lax.rem(n, 6) == role) & (n // 6 == half)))
            def _():
                take(kvs.at[k, :, 0], ks_s.at[k, n])

        def sent_kt(n):
            @pl.when(n != own + 8 * zh)
            def _():
                take(kvt.at[k, :, :, 0], kt_s.at[k, n])

        def sent_o(n):
            @pl.when((role < 6) & (n != src))
            def _():
                take(oss.at[k, 0], os_s.at[k, n])

            @pl.when(n != own)
            def _():
                take(ots.at[k, 0], ot_s.at[k, n])

        loop(12, sent_ks)
        loop(16, sent_kt)
        loop(8, sent_o)

    def sent_last(n):
        @pl.when((n < 6) & (n != role))
        def _():
            take(qs.at[STEPS - 1, 0], qs_s.at[STEPS - 1, n])

        @pl.when(n != own)
        def _():
            take(qt.at[STEPS - 1, :, 0], qt_s.at[STEPS - 1, n])

    loop(8, sent_last)


def per_device(latent, timesteps, w_qkv, w_out, w_time, stale_kv):
    anywhere = pl.BlockSpec(memory_space=pl.ANY)
    dma = pltpu.SemaphoreType.DMA
    x_out, vel, next_kv = pl.pallas_call(
        kernel,
        out_shape=[
            jax.ShapeDtypeStruct((ROWS, WIDTH), BF16),
            jax.ShapeDtypeStruct((ROWS, WIDTH), BF16),
            jax.ShapeDtypeStruct((2, D, WIDTH), BF16),
        ],
        in_specs=[pl.BlockSpec(memory_space=pltpu.SMEM)] + [anywhere] * 5,
        out_specs=[anywhere] * 3,
        scratch_shapes=[
            pltpu.VMEM((ROWS, WIDTH), BF16),
            pltpu.VMEM((ROWS, WIDTH), BF16),
            pltpu.VMEM((ROWS, WIDTH), BF16),
            pltpu.VMEM((WIDTH, 2304), BF16),
            pltpu.VMEM((QW, WIDTH), BF16),
            pltpu.VMEM((FREQ, 3 * WIDTH), BF16),
            pltpu.VMEM((8, 3 * WIDTH), F32),
            pltpu.VMEM((6, 2, D, D), BF16),
            pltpu.VMEM((3, 4, 3, 2, D, D), BF16),
            pltpu.VMEM((2, 2, 16, D, D), BF16),
            pltpu.VMEM((2, 2, 3, 16, 2, 16, D), BF16),
            pltpu.VMEM((2, 8, D, D), BF16),
            pltpu.VMEM((2, 3, 8, 2, 16, D), BF16),
            pltpu.VMEM((2, 8, D + 16, D), BF16),
            pltpu.VMEM((2, 6, D + 16, D), BF16),
            pltpu.VMEM((2, 8, 112, D), BF16),
            pltpu.VMEM((2, 8, 112, D), BF16),
            pltpu.VMEM((2 * D, 16 * D), F32),
            pltpu.VMEM((6, D, D), F32),
            pltpu.VMEM((6, D, 1), F32),
            pltpu.VMEM((3, 2, D, D), F32),
            pltpu.VMEM((3, 2, D, 1), F32),
            pltpu.VMEM((ROWS, QW), BF16),
            dma((4,)), dma((12,)), dma((2, 6)), dma((12,)),
            dma((2, 12)), dma((2, 16)), dma((2, 16)), dma((2, 16)),
            dma((2, 6)), dma((2, 8)), dma((2, 8)), dma((2, 8)),
            dma((2, 8)), dma((2, 6)), dma((2, 8)), dma((2, 8)),
        ],
        compiler_params=pltpu.CompilerParams(
            collective_id=0, has_side_effects=True, vmem_limit_bytes=50 * 2**20),
        cost_estimate=pl.CostEstimate(
            flops=8_000_000_000, bytes_accessed=18_000_000, transcendentals=5_000_000),
    )(timesteps, latent.reshape(ROWS, WIDTH), stale_kv, w_qkv, w_out, w_time)
    shape = (2, D, WIDTH)
    return x_out.reshape(shape), vel.reshape(shape), next_kv


def solution(mesh):
    tokens = P("frame", "patch", None)
    return jax.shard_map(
        per_device,
        mesh=mesh,
        in_specs=(tokens, P(), P(), P(), P(), tokens),
        out_specs=(tokens, tokens, tokens),
        check_vma=False,
    )
```

```python
import functools
import math

import jax
import jax.numpy as jnp
from jax import lax
from jax.experimental import pallas as pl
from jax.experimental.pallas import tpu as pltpu
from jax.sharding import PartitionSpec as P

MESH = pl.DeviceIdType.MESH
D = 128
SH = 3
TH = 3
WIDTH = 1536
QW = (SH + TH) * D
ROWS = 256
FREQ = 256
STEPS = 2
NEG = -1e30
LOG2 = math.log2(math.e) / math.sqrt(D)
F32 = jnp.float32
BF16 = jnp.bfloat16


def dot_t(a, b):
    return lax.dot_general(a, b, (((1,), (1,)), ((), ())), preferred_element_type=F32)


def iota(shape, dim):
    return lax.broadcasted_iota(jnp.int32, shape, dim)


def split3(value):
    hi = value.astype(BF16).astype(F32)
    mid = (value - hi).astype(BF16).astype(F32)
    return hi, mid, value - hi - mid


def col_to_row(col):
    eye = iota((D, D), 0) == iota((D, D), 1)
    return jnp.sum(jnp.where(eye, col, 0.0), axis=0, keepdims=True)


def sigma_of(index):
    unit = index.astype(F32) / 1000.0
    return 5.0 * unit / (1.0 + 4.0 * unit)


def kernel(
    ts_ref, lat_ref, stale_ref, wqkv_ref, wout_ref, wtime_ref,
    xo_ref, vo_ref, kvo_ref,
    x_v, h_v, vel_v, part_v, wqkv_v, wout_v, wtime_v, mods_v,
    qloc, kvloc, kvs, kvt, qs, qt, oss, osr, ots, otr,
    s_v, p_v, inv_v, ol_s, ll_s, ol_t, ll_t, att,
    load_sem, stale_sem, out_sem, kvo_sem,
    ks_s, ks_r, kt_s, kt_r, qs_s, qs_r, qt_s, qt_r, os_s, os_r, ot_s, ot_r,
):
    fi = lax.axis_index("frame")
    pi = lax.axis_index("patch")
    core = lax.rem(fi, 2)
    zh = lax.rem(fi // 2, 2)
    own = (fi // 4) * 2 + core
    half = lax.rem(pi, 4) // 2
    src = (pi // 4) * 2 + lax.rem(pi, 2)
    role = lax.rem(src + 4 * core, 8)

    def patch_at(place, of_half):
        return (place // 2) * 4 + 2 * of_half + lax.rem(place, 2)

    def place_of(pair):
        return lax.rem(pair + 8 - 4 * core, 8)

    def frame_at(owner, group):
        return (owner // 2) * 4 + group * 2 + lax.rem(owner, 2)

    def push(source, target, send, recv, device, is_self):
        @pl.when(is_self)
        def _():
            pltpu.make_async_copy(source, target, recv).start()

        @pl.when(jnp.logical_not(is_self))
        def _():
            pltpu.make_async_remote_copy(
                src_ref=source, dst_ref=target, send_sem=send, recv_sem=recv,
                device_id=device, device_id_type=MESH,
            ).start()

    def take(ref, sem):
        pltpu.make_async_copy(ref, ref, sem).wait()

    def take_sent(all_of_them, but_one, sem):
        @pl.when(role < 6)
        def _():
            take(but_one, sem)

        @pl.when(role >= 6)
        def _():
            take(all_of_them, sem)

    def loop(count, body):
        def step(index, carry):
            body(index)
            return carry
        lax.fori_loop(0, count, step, 0)

    def load_stale(block):
        return pltpu.make_async_copy(
            stale_ref.at[:, :, pl.ds(pl.multiple_of(block * D, D), D)],
            kvloc.at[0, block // 3, lax.rem(block, 3)], stale_sem.at[block])

    loop(12, lambda b: load_stale(b).start())
    loads = [
        pltpu.make_async_copy(a, b, load_sem.at[n])
        for n, (a, b) in enumerate(
            [(lat_ref, x_v), (wtime_ref, wtime_v), (wqkv_ref, wqkv_v), (wout_ref, wout_v)])
    ]
    for one in loads:
        one.start()

    barrier = pltpu.get_barrier_semaphore()

    def greet(k):
        pl.semaphore_signal(
            barrier, inc=1, device_id=(fi, lax.rem(pi + k + 1, 16)), device_id_type=MESH)
        pl.semaphore_signal(
            barrier, inc=1, device_id=(lax.rem(fi + k + 1, 16), pi), device_id_type=MESH)

    loop(15, greet)
    loop(12, lambda b: load_stale(b).wait())
    pl.semaphore_wait(barrier, 30)

    def send_spatial(k, kv):
        def one(n):
            to_half = lax.rem(half + 1 + n // 6, 2)
            pair = lax.rem(n, 6)
            frame, head = pair // 3, lax.rem(pair, 3)
            device = patch_at(place_of(pair), to_half)
            slot = src + 8 * jnp.where(to_half == half, 0, 1)
            push(kvloc.at[k, kv, head, frame], kvs.at[k, kv, slot], ks_s.at[k, kv], ks_r.at[k, kv],
                 (fi, device), device == pi)

        loop(12, one)

    def send_temporal(k):
        def one(n):
            group = lax.rem(zh + 1 + n // 8, 2)
            owner = lax.rem(n + own, 8)
            device = frame_at(owner, group)
            slot = own + 8 * jnp.where(group == zh, 0, 1)
            rows = pl.ds(pl.multiple_of(owner * 16, 16), 16)
            push(kvloc.at[k, 2:4, :, :, rows], kvt.at[k, :, :, slot], kt_s.at[k], kt_r.at[k],
                 (device, pi), device == fi)

        loop(16, one)

    send_temporal(0)
    send_spatial(0, 0)

    loads[1].wait()
    lane = iota((16, D), 1).astype(F32)
    row = iota((16, D), 0)
    level = jnp.where(
        row < 3, sigma_of(jnp.full((16, D), ts_ref[0], jnp.int32)),
        sigma_of(jnp.full((16, D), ts_ref[1], jnp.int32))) * 1000.0
    angles = level * jnp.exp(-math.log(10000.0) * lane / D)
    part = lax.rem(row, 3)

    def embed(value):
        value = value / (1.0 + jnp.exp(-value))
        hi, mid, low = split3(value)
        return jnp.where(part == 0, hi, jnp.where(part == 1, mid, low)).astype(BF16)

    emb = jnp.concatenate([embed(jnp.cos(angles)), embed(jnp.sin(angles))], axis=1)
    for n in range(0, 3 * WIDTH, 512):
        cols = slice(n, n + 512)
        parts = jnp.dot(emb, wtime_v[:, cols], preferred_element_type=F32)
        for k in range(STEPS):
            mods_v[k : k + 1, cols] = jnp.sum(parts[3 * k : 3 * k + 3], axis=0, keepdims=True)

    loads[0].wait()

    def sent_queries(k):
        take_sent(qs.at[k, 0:6], qs.at[k, 0:5], qs_s.at[k])
        take(qt.at[k, :, 0:7], qt_s.at[k])

    for k in range(STEPS):
        def norm(n):
            rows = pl.ds(pl.multiple_of(n * 32, 32), 32)
            value = x_v[rows, :].astype(F32)
            center = jnp.mean(value, axis=-1, keepdims=True)
            value = value - center
            spread = jnp.mean(value * value, axis=-1, keepdims=True)
            value = value * lax.rsqrt(spread + 1e-06)
            h_v[rows, :] = (
                value * (1.0 + mods_v[k : k + 1, WIDTH : 2 * WIDTH]) + mods_v[k : k + 1, :WIDTH]
            ).astype(BF16)

        loop(ROWS // 32, norm)
        if k == 0:
            loads[2].wait()

        def project(n):
            cols = pl.ds(pl.multiple_of(n * 256, 256), 256)
            return jnp.dot(h_v[...], wqkv_v[:, cols], preferred_element_type=F32).astype(BF16)

        def query(n):
            out = project(n)
            for part_n in range(2):
                qloc[2 * n + part_n] = out[:, part_n * D : (part_n + 1) * D].reshape(2, D, D)

        if k > 0:
            sent_queries(k - 1)
        loop(3, query)

        def send_q(pair):
            place = place_of(pair)
            frame, head = pair // 3, lax.rem(pair, 3)
            push(qloc.at[head, frame], qs.at[k, src], qs_s.at[k], qs_r.at[k],
                 (fi, patch_at(place, half)), place == src)

        def send_qt(owner):
            rows = pl.ds(pl.multiple_of(owner * 16, 16), 16)
            push(qloc.at[3:6, :, rows], qt.at[k, :, own], qt_s.at[k], qt_r.at[k],
                 (frame_at(owner, zh), pi), owner == own)

        loop(6, send_q)
        loop(8, send_qt)
        send_spatial(k, 1)

        def fresh(n):
            out = project(n + 3)
            for part_n in range(2):
                block = 2 * n + part_n
                kvloc[k + 1, block // 3, lax.rem(block, 3)] = out[:, part_n * D : (part_n + 1) * D].reshape(2, D, D)

        loop(6, fresh)

        def store_kv(block):
            return pltpu.make_async_copy(
                kvloc.at[STEPS, block // 3, lax.rem(block, 3)],
                kvo_ref.at[:, :, pl.ds(pl.multiple_of(block * D, D), D)], kvo_sem.at[block])

        if k + 1 == STEPS:
            loop(12, lambda b: store_kv(b).start())

        def local_spatial(pair):
            frame, head = pair // 3, pair % 3
            scores = dot_t(qloc[head, frame], kvloc[k + 1, 0, head, frame]) * LOG2
            top = jnp.max(scores, axis=-1, keepdims=True)
            expo = jnp.exp2(scores - top)
            total = jnp.sum(expo, axis=-1, keepdims=True)
            out = jnp.dot(expo.astype(BF16), kvloc[k + 1, 1, head, frame], preferred_element_type=F32)
            ol_s[pair] = out / total
            ll_s[pair] = top + jnp.log2(total)

        for pair in range(6):
            local_spatial(pair)

        def local_temporal(head):
            for frame in range(2):
                q = qloc[3 + head, frame].astype(F32)
                s0, s1 = [
                    jnp.sum(q * kvloc[k + 1, 2, head, f].astype(F32), axis=-1, keepdims=True) * LOG2
                    for f in range(2)
                ]
                top = jnp.maximum(s0, s1)
                e0, e1 = jnp.exp2(s0 - top), jnp.exp2(s1 - top)
                total = e0 + e1
                out = e0 * kvloc[k + 1, 3, head, 0].astype(F32) + e1 * kvloc[k + 1, 3, head, 1].astype(F32)
                ol_t[head, frame] = out / total
                ll_t[head, frame] = top + jnp.log2(total)

        for head in range(TH):
            local_temporal(head)

        take(qt.at[k], qt_r.at[k])
        take(kvt.at[k], kt_r.at[k])
        rows_i, cols_i = iota((ROWS, 2 * ROWS), 0), iota((ROWS, 2 * ROWS), 1)
        seen = (lax.rem(rows_i, 16) == lax.rem(cols_i, 16)) & (rows_i // 32 != cols_i // 32)
        tile = iota((16, D), 0)
        stats = [jnp.zeros((16, D), F32), jnp.zeros((16, D), F32)]
        for head in range(TH):
            scores = dot_t(qt[k, head].reshape(ROWS, D), kvt[k, 0, head].reshape(2 * ROWS, D))
            scores = jnp.where(seen, scores, NEG)
            top = jnp.max(scores, axis=-1, keepdims=True)
            expo = jnp.exp2((scores - top) * LOG2)
            total = jnp.sum(expo, axis=-1, keepdims=True)
            out = jnp.dot(
                expo.astype(BF16), kvt[k, 1, head].reshape(2 * ROWS, D), preferred_element_type=F32)
            out = (out / total).astype(BF16)
            lse = top * LOG2 + jnp.log2(total)
            ots[k, :, head * 32 : head * 32 + 32] = out.reshape(8, 32, D)
            for chunk in range(2):
                parts = split3(col_to_row(lse[chunk * D : (chunk + 1) * D]))
                for n, value in enumerate(parts):
                    stats[chunk] = jnp.where(tile == 3 * head + n, value, stats[chunk])
        for place in range(8):
            ots[k, place, 96:112] = stats[place // 4].astype(BF16)

        def send_ot(place):
            push(ots.at[k, place], otr.at[k, own], ot_s.at[k], ot_r.at[k],
                 (frame_at(place, zh), pi), place == own)

        loop(8, send_ot)
        if k + 1 < STEPS:
            send_spatial(k + 1, 0)

        @pl.when(role < 6)
        def _():
            take(qs.at[k], qs_r.at[k])
            take(kvs.at[k, 0], ks_r.at[k, 0])

            def weigh(n):
                q = qs[k, pl.ds(2 * n, 2)].reshape(2 * D, D)
                s_v[...] = dot_t(q, kvs[k, 0].reshape(16 * D, D))
                base = pl.multiple_of(n * 2 * D, 2 * D)
                s_v[0:D, pl.ds(base, D)] = jnp.full((D, D), NEG, F32)
                s_v[D : 2 * D, pl.ds(pl.multiple_of(base + D, D), D)] = jnp.full((D, D), NEG, F32)
                scores = s_v[...]
                top = jnp.max(scores, axis=-1, keepdims=True)
                expo = jnp.exp2((scores - top) * LOG2)
                total = jnp.sum(expo, axis=-1, keepdims=True)
                p_v[pl.ds(base, 2 * D), :] = expo.astype(BF16)
                inv_v[pl.ds(base, 2 * D), :] = 1.0 / total
                lse = top * LOG2 + jnp.log2(total)
                for part_n in range(2):
                    hi, mid, low = split3(col_to_row(lse[part_n * D : (part_n + 1) * D]))
                    tile = iota((16, D), 0)
                    oss[k, 2 * n + part_n, D : D + 16] = jnp.where(
                        tile == 0, hi, jnp.where(tile == 1, mid, jnp.where(tile == 2, low, 0.0))).astype(BF16)

            loop(4, weigh)

        def merge(mine, mine_lse, other, other_lse):
            weight = 1.0 / (1.0 + jnp.exp2(mine_lse - other_lse))
            return (mine + weight * (other.astype(F32) - mine)).astype(BF16)

        def columns(pick, stat, at):
            lse = dot_t(pick.astype(BF16), stat)
            return [jnp.sum(lse[:, c : c + 3], axis=-1, keepdims=True) for c in at]

        def finish_temporal():
            take(otr.at[k], ot_r.at[k])
            pick = iota((32, D), 1) == iota((32, D), 0) + 32 * lax.rem(own, 4)
            lse_t = columns(
                pick, otr[k, :, 96:112].reshape(8 * 16, D), [16 * o + 3 * h for o in range(8) for h in range(TH)])
            for owner in range(8):
                for head in range(TH):
                    for frame in range(2):
                        rows = slice(owner * 16, owner * 16 + 16)
                        att[frame * D + owner * 16 : frame * D + owner * 16 + 16, (SH + head) * D : (SH + head + 1) * D] = merge(
                            ol_t[head, frame, rows], ll_t[head, frame, rows],
                            otr[k, owner, head * 32 + frame * 16 : head * 32 + frame * 16 + 16],
                            lse_t[owner * TH + head][frame * 16 : frame * 16 + 16])
            if k == 0:
                loads[3].wait()

            def first_half(n):
                cols = pl.ds(pl.multiple_of(n * 256, 256), 256)
                part_v[:, cols] = jnp.dot(
                    att[:, SH * D :], wout_v[SH * D :, cols], preferred_element_type=F32)

            loop(WIDTH // 256, first_half)

        if k + 1 == STEPS:
            finish_temporal()

        @pl.when(role < 6)
        def _():
            take(kvs.at[k, 1], ks_r.at[k, 1])

            def attend(turn):
                n = lax.rem(turn + role, 4)
                rows = pl.ds(pl.multiple_of(n * 2 * D, 2 * D), 2 * D)
                out = jnp.dot(p_v[rows, :], kvs[k, 1].reshape(16 * D, D), preferred_element_type=F32)
                out = (out * inv_v[rows, :]).astype(BF16)
                for part_n in range(2):
                    place = 2 * n + part_n
                    oss[k, place, 0:D] = out[part_n * D : (part_n + 1) * D]
                    push(oss.at[k, place], osr.at[k, role], os_s.at[k], os_r.at[k],
                         (fi, patch_at(place, half)), place == src)

            loop(4, attend)

        if k + 1 < STEPS:
            send_temporal(k + 1)
            finish_temporal()

        take(osr.at[k], os_r.at[k])
        lse_s = columns(
            iota((D, D), 0) == iota((D, D), 1), osr[k, :, D : D + 16].reshape(6 * 16, D), [16 * p for p in range(6)])
        for pair in range(6):
            frame, head = pair // 3, pair % 3
            att[frame * D : (frame + 1) * D, head * D : (head + 1) * D] = merge(
                ol_s[pair], ll_s[pair], osr[k, pair, 0:D], lse_s[pair])

        dsig = (sigma_of(jnp.full((1, 256), ts_ref[k + 1], jnp.int32))
                - sigma_of(jnp.full((1, 256), ts_ref[k], jnp.int32)))

        def stores(n):
            cols = pl.ds(pl.multiple_of(n * 256, 256), 256)
            return [
                pltpu.make_async_copy(x_v.at[:, cols], xo_ref.at[:, cols], out_sem.at[0, n]),
                pltpu.make_async_copy(vel_v.at[:, cols], vo_ref.at[:, cols], out_sem.at[1, n]),
            ]

        def update(n):
            cols = pl.ds(pl.multiple_of(n * 256, 256), 256)
            branch = part_v[:, cols] + jnp.dot(
                att[:, : SH * D], wout_v[: SH * D, cols], preferred_element_type=F32)
            vel = mods_v[k : k + 1, pl.ds(pl.multiple_of(2 * WIDTH + n * 256, 256), 256)] * branch
            x_v[:, cols] = (x_v[:, cols].astype(F32) + dsig * vel).astype(BF16)
            if k + 1 == STEPS:
                vel_v[:, cols] = vel.astype(BF16)
                for one in stores(n):
                    one.start()

        loop(WIDTH // 256, update)

    for k in range(STEPS):
        for kv in range(2):
            take_sent(kvs.at[k, kv, 0:12], kvs.at[k, kv, 0:11], ks_s.at[k, kv])
        take(kvt.at[k, :, :, 0:15], kt_s.at[k])

        @pl.when(role < 6)
        def _():
            take(oss.at[k, 0:7], os_s.at[k])

        take(ots.at[k, 0:7], ot_s.at[k])
    sent_queries(STEPS - 1)
    loop(12, lambda b: store_kv(b).wait())

    def stored(n):
        for one in stores(n):
            one.wait()

    loop(WIDTH // 256, stored)


def hand_on(a_ref, b_ref, c_ref, ao_ref, bo_ref, co_ref, a_v, b_v, c_v, in_sem, out_sem):
    moves = [
        (pltpu.make_async_copy(a, v, in_sem.at[n]), pltpu.make_async_copy(v, b, out_sem.at[n]))
        for n, (a, v, b) in enumerate([(a_ref, a_v, ao_ref), (b_ref, b_v, bo_ref), (c_ref, c_v, co_ref)])
    ]
    for into, _ in moves:
        into.start()
    for into, out in moves:
        into.wait()
        out.start()
    for _, out in moves:
        out.wait()


def per_device(latent, timesteps, w_qkv, w_out, w_time, stale_kv):
    anywhere = pl.BlockSpec(memory_space=pl.ANY)
    dma = pltpu.SemaphoreType.DMA
    results = [
        jax.ShapeDtypeStruct((ROWS, WIDTH), BF16),
        jax.ShapeDtypeStruct((ROWS, WIDTH), BF16),
        jax.ShapeDtypeStruct((2, D, WIDTH), BF16),
    ]
    made = pl.pallas_call(
        kernel,
        out_shape=results,
        in_specs=[pl.BlockSpec(memory_space=pltpu.SMEM)] + [anywhere] * 5,
        out_specs=[anywhere] * 3,
        scratch_shapes=[
            pltpu.VMEM((ROWS, WIDTH), BF16),
            pltpu.VMEM((ROWS, WIDTH), BF16),
            pltpu.VMEM((ROWS, WIDTH), BF16),
            pltpu.VMEM((ROWS, WIDTH), F32),
            pltpu.VMEM((WIDTH, 2304), BF16),
            pltpu.VMEM((QW, WIDTH), BF16),
            pltpu.VMEM((FREQ, 3 * WIDTH), BF16),
            pltpu.VMEM((8, 3 * WIDTH), F32),
            pltpu.VMEM((6, 2, D, D), BF16),
            pltpu.VMEM((3, 4, 3, 2, D, D), BF16),
            pltpu.VMEM((2, 2, 16, D, D), BF16),
            pltpu.VMEM((2, 2, 3, 16, 2, 16, D), BF16),
            pltpu.VMEM((2, 8, D, D), BF16),
            pltpu.VMEM((2, 3, 8, 2, 16, D), BF16),
            pltpu.VMEM((2, 8, D + 16, D), BF16),
            pltpu.VMEM((2, 6, D + 16, D), BF16),
            pltpu.VMEM((2, 8, 112, D), BF16),
            pltpu.VMEM((2, 8, 112, D), BF16),
            pltpu.VMEM((2 * D, 16 * D), F32),
            pltpu.VMEM((8 * D, 16 * D), BF16),
            pltpu.VMEM((8 * D, 1), F32),
            pltpu.VMEM((6, D, D), F32),
            pltpu.VMEM((6, D, 1), F32),
            pltpu.VMEM((3, 2, D, D), F32),
            pltpu.VMEM((3, 2, D, 1), F32),
            pltpu.VMEM((ROWS, QW), BF16),
            dma((4,)), dma((12,)), dma((2, 6)), dma((12,)),
            dma((2, 2)), dma((2, 2)), dma((2,)), dma((2,)),
            dma((2,)), dma((2,)), dma((2,)), dma((2,)),
            dma((2,)), dma((2,)), dma((2,)), dma((2,)),
        ],
        compiler_params=pltpu.CompilerParams(
            collective_id=0, has_side_effects=True, vmem_limit_bytes=62 * 2**20),
        cost_estimate=pl.CostEstimate(
            flops=8_000_000_000, bytes_accessed=18_000_000, transcendentals=5_000_000),
    )(timesteps, latent.reshape(ROWS, WIDTH), stale_kv, w_qkv, w_out, w_time)
    x_out, vel, next_kv = pl.pallas_call(
        hand_on,
        out_shape=results,
        in_specs=[anywhere] * 3,
        out_specs=[anywhere] * 3,
        scratch_shapes=[pltpu.VMEM(one.shape, BF16) for one in results] + [dma((3,)), dma((3,))],
        compiler_params=pltpu.CompilerParams(vmem_limit_bytes=60 * 2**20),
    )(*made)
    shape = (2, D, WIDTH)
    return x_out.reshape(shape), vel.reshape(shape), next_kv


def solution(mesh):
    tokens = P("frame", "patch", None)
    return jax.shard_map(
        per_device,
        mesh=mesh,
        in_specs=(tokens, P(), P(), P(), P(), tokens),
        out_specs=(tokens, tokens, tokens),
        check_vma=False,
    )
```

```python
import functools
import math

import jax
import jax.numpy as jnp
from jax import lax
from jax.experimental import pallas as pl
from jax.experimental.pallas import tpu as pltpu
from jax.sharding import PartitionSpec as P

MESH = pl.DeviceIdType.MESH
D = 128
SH = 3
TH = 3
WIDTH = 1536
QW = (SH + TH) * D
ROWS = 256
FREQ = 256
STEPS = 2
NEG = -1e30
LOG2 = math.log2(math.e) / math.sqrt(D)
F32 = jnp.float32
BF16 = jnp.bfloat16


def dot_t(a, b):
    return lax.dot_general(a, b, (((1,), (1,)), ((), ())), preferred_element_type=F32)


def iota(shape, dim):
    return lax.broadcasted_iota(jnp.int32, shape, dim)


def split3(value):
    hi = value.astype(BF16).astype(F32)
    mid = (value - hi).astype(BF16).astype(F32)
    return hi, mid, value - hi - mid


def col_to_row(col):
    eye = iota((D, D), 0) == iota((D, D), 1)
    return jnp.sum(jnp.where(eye, col, 0.0), axis=0, keepdims=True)


def sigma_of(index):
    unit = index.astype(F32) / 1000.0
    return 5.0 * unit / (1.0 + 4.0 * unit)


def kernel(
    ts_ref, lat_ref, stale_ref, wqkv_ref, wout_ref, wtime_ref,
    xo_ref, vo_ref, kvo_ref,
    x_v, h_v, vel_v, part_v, wqkv_v, wout_v, wtime_v, mods_v,
    qloc, kvloc, kvs, kvt, qs, qt, oss, osr, ots, otr,
    s_v, p_v, inv_v, ol_s, ll_s, ol_t, ll_t, att,
    load_sem, stale_sem, out_sem, kvo_sem,
    ks_s, ks_r, kt_s, kt_r, qs_s, qs_r, qt_s, qt_r, os_s, os_r, ot_s, ot_r,
):
    fi = lax.axis_index("frame")
    pi = lax.axis_index("patch")
    core = lax.rem(fi, 2)
    zh = lax.rem(fi // 2, 2)
    own = (fi // 4) * 2 + core
    half = lax.rem(pi, 4) // 2
    src = (pi // 4) * 2 + lax.rem(pi, 2)
    role = lax.rem(src + 4 * core, 8)

    def patch_at(place, of_half):
        return (place // 2) * 4 + 2 * of_half + lax.rem(place, 2)

    def place_of(pair):
        return lax.rem(pair + 8 - 4 * core, 8)

    def frame_at(owner, group):
        return (owner // 2) * 4 + group * 2 + lax.rem(owner, 2)

    def push(source, target, send, recv, device, is_self):
        @pl.when(is_self)
        def _():
            pltpu.make_async_copy(source, target, recv).start()

        @pl.when(jnp.logical_not(is_self))
        def _():
            pltpu.make_async_remote_copy(
                src_ref=source, dst_ref=target, send_sem=send, recv_sem=recv,
                device_id=device, device_id_type=MESH,
            ).start()

    def take(ref, sem):
        pltpu.make_async_copy(ref, ref, sem).wait()

    def take_sent(all_of_them, but_one, sem):
        @pl.when(role < 6)
        def _():
            take(but_one, sem)

        @pl.when(role >= 6)
        def _():
            take(all_of_them, sem)

    def loop(count, body):
        def step(index, carry):
            body(index)
            return carry
        lax.fori_loop(0, count, step, 0)

    barrier = pltpu.get_barrier_semaphore()

    def greet(k):
        pl.semaphore_signal(
            barrier, inc=1, device_id=(fi, lax.rem(pi + k + 1, 16)), device_id_type=MESH)
        pl.semaphore_signal(
            barrier, inc=1, device_id=(lax.rem(fi + k + 1, 16), pi), device_id_type=MESH)

    loop(15, greet)

    def load_stale(block):
        return pltpu.make_async_copy(
            stale_ref.at[:, :, pl.ds(pl.multiple_of(block * D, D), D)],
            kvloc.at[0, block // 3, lax.rem(block, 3)], stale_sem.at[block])

    loop(12, lambda b: load_stale(b).start())
    loads = [
        pltpu.make_async_copy(a, b, load_sem.at[n])
        for n, (a, b) in enumerate(
            [(lat_ref, x_v), (wtime_ref, wtime_v), (wqkv_ref, wqkv_v), (wout_ref, wout_v)])
    ]
    for one in loads:
        one.start()

    loop(12, lambda b: load_stale(b).wait())
    pl.semaphore_wait(barrier, 30)

    def send_spatial(k, kv):
        def one(n):
            to_half = lax.rem(half + 1 + n // 6, 2)
            pair = lax.rem(n, 6)
            frame, head = pair // 3, lax.rem(pair, 3)
            device = patch_at(place_of(pair), to_half)
            slot = src + 8 * jnp.where(to_half == half, 0, 1)
            push(kvloc.at[k, kv, head, frame], kvs.at[k, kv, slot], ks_s.at[k, kv], ks_r.at[k, kv],
                 (fi, device), device == pi)

        loop(12, one)

    def send_temporal(k, first, count):
        def one(turn):
            n = first + turn
            group = lax.rem(zh + 1 + n, 2)
            owner = lax.rem(n // 2 + own, 8)
            device = frame_at(owner, group)
            slot = own + 8 * jnp.where(group == zh, 0, 1)
            rows = pl.ds(pl.multiple_of(owner * 16, 16), 16)
            push(kvloc.at[k, 2:4, :, :, rows], kvt.at[k, :, :, slot], kt_s.at[k], kt_r.at[k],
                 (device, pi), device == fi)

        loop(count, one)

    send_spatial(0, 0)

    loads[1].wait()
    lane = iota((16, D), 1).astype(F32)
    row = iota((16, D), 0)
    level = jnp.where(
        row < 3, sigma_of(jnp.full((16, D), ts_ref[0], jnp.int32)),
        sigma_of(jnp.full((16, D), ts_ref[1], jnp.int32))) * 1000.0
    angles = level * jnp.exp(-math.log(10000.0) * lane / D)
    part = lax.rem(row, 3)

    def embed(value):
        value = value / (1.0 + jnp.exp(-value))
        hi, mid, low = split3(value)
        return jnp.where(part == 0, hi, jnp.where(part == 1, mid, low)).astype(BF16)

    emb = jnp.concatenate([embed(jnp.cos(angles)), embed(jnp.sin(angles))], axis=1)
    for n in range(0, 3 * WIDTH, 512):
        cols = slice(n, n + 512)
        parts = jnp.dot(emb, wtime_v[:, cols], preferred_element_type=F32)
        for k in range(STEPS):
            mods_v[k : k + 1, cols] = jnp.sum(parts[3 * k : 3 * k + 3], axis=0, keepdims=True)

    loads[0].wait()

    def sent_queries(k):
        take_sent(qs.at[k, 0:6], qs.at[k, 0:5], qs_s.at[k])
        take(qt.at[k, :, 0:7], qt_s.at[k])

    for k in range(STEPS):
        def norm(n):
            rows = pl.ds(pl.multiple_of(n * 32, 32), 32)
            value = x_v[rows, :].astype(F32)
            center = jnp.mean(value, axis=-1, keepdims=True)
            value = value - center
            spread = jnp.mean(value * value, axis=-1, keepdims=True)
            value = value * lax.rsqrt(spread + 1e-06)
            h_v[rows, :] = (
                value * (1.0 + mods_v[k : k + 1, WIDTH : 2 * WIDTH]) + mods_v[k : k + 1, :WIDTH]
            ).astype(BF16)

        loop(ROWS // 32, norm)
        if k == 0:
            loads[2].wait()

        def project(n):
            cols = pl.ds(pl.multiple_of(n * 256, 256), 256)
            return jnp.dot(h_v[...], wqkv_v[:, cols], preferred_element_type=F32).astype(BF16)

        def query(n):
            out = project(n)
            for part_n in range(2):
                qloc[2 * n + part_n] = out[:, part_n * D : (part_n + 1) * D].reshape(2, D, D)

        if k > 0:
            sent_queries(k - 1)
        loop(3, query)

        def send_q(pair):
            place = place_of(pair)
            frame, head = pair // 3, lax.rem(pair, 3)
            push(qloc.at[head, frame], qs.at[k, src], qs_s.at[k], qs_r.at[k],
                 (fi, patch_at(place, half)), place == src)

        def send_qt(owner):
            rows = pl.ds(pl.multiple_of(owner * 16, 16), 16)
            push(qloc.at[3:6, :, rows], qt.at[k, :, own], qt_s.at[k], qt_r.at[k],
                 (frame_at(owner, zh), pi), owner == own)

        loop(6, send_q)
        loop(8, send_qt)
        if k == 0:
            send_spatial(0, 1)
            send_temporal(0, 0, 16)
        else:
            send_temporal(1, 8, 8)

        def fresh(n):
            out = project(n + 3)
            for part_n in range(2):
                block = 2 * n + part_n
                kvloc[k + 1, block // 3, lax.rem(block, 3)] = out[:, part_n * D : (part_n + 1) * D].reshape(2, D, D)

        loop(6, fresh)

        def store_kv(block):
            return pltpu.make_async_copy(
                kvloc.at[STEPS, block // 3, lax.rem(block, 3)],
                kvo_ref.at[:, :, pl.ds(pl.multiple_of(block * D, D), D)], kvo_sem.at[block])

        if k + 1 == STEPS:
            loop(12, lambda b: store_kv(b).start())

        def local_spatial(pair):
            frame, head = pair // 3, pair % 3
            scores = dot_t(qloc[head, frame], kvloc[k + 1, 0, head, frame]) * LOG2
            top = jnp.max(scores, axis=-1, keepdims=True)
            expo = jnp.exp2(scores - top)
            total = jnp.sum(expo, axis=-1, keepdims=True)
            out = jnp.dot(expo.astype(BF16), kvloc[k + 1, 1, head, frame], preferred_element_type=F32)
            ol_s[pair] = out / total
            ll_s[pair] = top + jnp.log2(total)

        for pair in range(6):
            local_spatial(pair)

        def local_temporal(head):
            for frame in range(2):
                q = qloc[3 + head, frame].astype(F32)
                s0, s1 = [
                    jnp.sum(q * kvloc[k + 1, 2, head, f].astype(F32), axis=-1, keepdims=True) * LOG2
                    for f in range(2)
                ]
                top = jnp.maximum(s0, s1)
                e0, e1 = jnp.exp2(s0 - top), jnp.exp2(s1 - top)
                total = e0 + e1
                out = e0 * kvloc[k + 1, 3, head, 0].astype(F32) + e1 * kvloc[k + 1, 3, head, 1].astype(F32)
                ol_t[head, frame] = out / total
                ll_t[head, frame] = top + jnp.log2(total)

        for head in range(TH):
            local_temporal(head)

        @pl.when(role < 6)
        def _():
            take(qs.at[k], qs_r.at[k])
            take(kvs.at[k, 0], ks_r.at[k, 0])

            def weigh(n):
                q = qs[k, pl.ds(2 * n, 2)].reshape(2 * D, D)
                s_v[...] = dot_t(q, kvs[k, 0].reshape(16 * D, D))
                base = pl.multiple_of(n * 2 * D, 2 * D)
                s_v[0:D, pl.ds(base, D)] = jnp.full((D, D), NEG, F32)
                s_v[D : 2 * D, pl.ds(pl.multiple_of(base + D, D), D)] = jnp.full((D, D), NEG, F32)
                scores = s_v[...]
                top = jnp.max(scores, axis=-1, keepdims=True)
                expo = jnp.exp2((scores - top) * LOG2)
                total = jnp.sum(expo, axis=-1, keepdims=True)
                p_v[pl.ds(base, 2 * D), :] = expo.astype(BF16)
                inv_v[pl.ds(base, 2 * D), :] = 1.0 / total
                lse = top * LOG2 + jnp.log2(total)
                for part_n in range(2):
                    hi, mid, low = split3(col_to_row(lse[part_n * D : (part_n + 1) * D]))
                    tile = iota((16, D), 0)
                    oss[k, 2 * n + part_n, D : D + 16] = jnp.where(
                        tile == 0, hi, jnp.where(tile == 1, mid, jnp.where(tile == 2, low, 0.0))).astype(BF16)

            loop(4, weigh)

        @pl.when(role < 6)
        def _():
            take(kvs.at[k, 1], ks_r.at[k, 1])

            def attend(turn):
                n = lax.rem(turn + role, 4)
                rows = pl.ds(pl.multiple_of(n * 2 * D, 2 * D), 2 * D)
                out = jnp.dot(p_v[rows, :], kvs[k, 1].reshape(16 * D, D), preferred_element_type=F32)
                out = (out * inv_v[rows, :]).astype(BF16)
                for part_n in range(2):
                    place = 2 * n + part_n
                    oss[k, place, 0:D] = out[part_n * D : (part_n + 1) * D]
                    push(oss.at[k, place], osr.at[k, role], os_s.at[k], os_r.at[k],
                         (fi, patch_at(place, half)), place == src)

            loop(4, attend)

        if k + 1 < STEPS:
            send_spatial(1, 0)
            send_spatial(1, 1)

        take(qt.at[k], qt_r.at[k])
        take(kvt.at[k], kt_r.at[k])
        rows_i, cols_i = iota((ROWS, 2 * ROWS), 0), iota((ROWS, 2 * ROWS), 1)
        seen = (lax.rem(rows_i, 16) == lax.rem(cols_i, 16)) & (rows_i // 32 != cols_i // 32)
        tile = iota((16, D), 0)
        stats = [jnp.zeros((16, D), F32), jnp.zeros((16, D), F32)]
        for head in range(TH):
            scores = dot_t(qt[k, head].reshape(ROWS, D), kvt[k, 0, head].reshape(2 * ROWS, D))
            scores = jnp.where(seen, scores, NEG)
            top = jnp.max(scores, axis=-1, keepdims=True)
            expo = jnp.exp2((scores - top) * LOG2)
            total = jnp.sum(expo, axis=-1, keepdims=True)
            out = jnp.dot(
                expo.astype(BF16), kvt[k, 1, head].reshape(2 * ROWS, D), preferred_element_type=F32)
            out = (out / total).astype(BF16)
            lse = top * LOG2 + jnp.log2(total)
            ots[k, :, head * 32 : head * 32 + 32] = out.reshape(8, 32, D)
            for chunk in range(2):
                parts = split3(col_to_row(lse[chunk * D : (chunk + 1) * D]))
                for n, value in enumerate(parts):
                    stats[chunk] = jnp.where(tile == 3 * head + n, value, stats[chunk])
        for place in range(8):
            ots[k, place, 96:112] = stats[place // 4].astype(BF16)

        def send_ot(place):
            push(ots.at[k, place], otr.at[k, own], ot_s.at[k], ot_r.at[k],
                 (frame_at(place, zh), pi), place == own)

        loop(8, send_ot)

        if k + 1 < STEPS:
            send_temporal(1, 0, 8)

        def merge(mine, mine_lse, other, other_lse):
            weight = 1.0 / (1.0 + jnp.exp2(mine_lse - other_lse))
            return (mine + weight * (other.astype(F32) - mine)).astype(BF16)

        def columns(pick, stat, at):
            lse = dot_t(pick.astype(BF16), stat)
            return [jnp.sum(lse[:, c : c + 3], axis=-1, keepdims=True) for c in at]

        take(osr.at[k], os_r.at[k])
        lse_s = columns(
            iota((D, D), 0) == iota((D, D), 1), osr[k, :, D : D + 16].reshape(6 * 16, D), [16 * p for p in range(6)])
        for pair in range(6):
            frame, head = pair // 3, pair % 3
            att[frame * D : (frame + 1) * D, head * D : (head + 1) * D] = merge(
                ol_s[pair], ll_s[pair], osr[k, pair, 0:D], lse_s[pair])

        if k == 0:
            loads[3].wait()

        def first_half(n):
            cols = pl.ds(pl.multiple_of(n * 256, 256), 256)
            part_v[:, cols] = jnp.dot(
                att[:, : SH * D], wout_v[: SH * D, cols], preferred_element_type=F32)

        loop(WIDTH // 256, first_half)

        take(otr.at[k], ot_r.at[k])
        pick = iota((32, D), 1) == iota((32, D), 0) + 32 * lax.rem(own, 4)
        lse_t = columns(
            pick, otr[k, :, 96:112].reshape(8 * 16, D), [16 * o + 3 * h for o in range(8) for h in range(TH)])
        for owner in range(8):
            for head in range(TH):
                for frame in range(2):
                    rows = slice(owner * 16, owner * 16 + 16)
                    att[frame * D + owner * 16 : frame * D + owner * 16 + 16, (SH + head) * D : (SH + head + 1) * D] = merge(
                        ol_t[head, frame, rows], ll_t[head, frame, rows],
                        otr[k, owner, head * 32 + frame * 16 : head * 32 + frame * 16 + 16],
                        lse_t[owner * TH + head][frame * 16 : frame * 16 + 16])

        dsig = (sigma_of(jnp.full((1, 256), ts_ref[k + 1], jnp.int32))
                - sigma_of(jnp.full((1, 256), ts_ref[k], jnp.int32)))

        def stores(n):
            cols = pl.ds(pl.multiple_of(n * 256, 256), 256)
            return [
                pltpu.make_async_copy(x_v.at[:, cols], xo_ref.at[:, cols], out_sem.at[0, n]),
                pltpu.make_async_copy(vel_v.at[:, cols], vo_ref.at[:, cols], out_sem.at[1, n]),
            ]

        def update(n):
            cols = pl.ds(pl.multiple_of(n * 256, 256), 256)
            branch = part_v[:, cols] + jnp.dot(
                att[:, SH * D :], wout_v[SH * D :, cols], preferred_element_type=F32)
            vel = mods_v[k : k + 1, pl.ds(pl.multiple_of(2 * WIDTH + n * 256, 256), 256)] * branch
            x_v[:, cols] = (x_v[:, cols].astype(F32) + dsig * vel).astype(BF16)
            if k + 1 == STEPS:
                vel_v[:, cols] = vel.astype(BF16)
                for one in stores(n):
                    one.start()

        loop(WIDTH // 256, update)

    for k in range(STEPS):
        for kv in range(2):
            take_sent(kvs.at[k, kv, 0:12], kvs.at[k, kv, 0:11], ks_s.at[k, kv])
        take(kvt.at[k, :, :, 0:15], kt_s.at[k])

        @pl.when(role < 6)
        def _():
            take(oss.at[k, 0:7], os_s.at[k])

        take(ots.at[k, 0:7], ot_s.at[k])
    sent_queries(STEPS - 1)
    loop(12, lambda b: store_kv(b).wait())

    def stored(n):
        for one in stores(n):
            one.wait()

    loop(WIDTH // 256, stored)


def hand_on(a_ref, b_ref, c_ref, ao_ref, bo_ref, co_ref, a_v, b_v, c_v, in_sem, out_sem):
    moves = [
        (pltpu.make_async_copy(a, v, in_sem.at[n]), pltpu.make_async_copy(v, b, out_sem.at[n]))
        for n, (a, v, b) in enumerate([(a_ref, a_v, ao_ref), (b_ref, b_v, bo_ref), (c_ref, c_v, co_ref)])
    ]
    for into, _ in moves:
        into.start()
    for into, out in moves:
        into.wait()
        out.start()
    for _, out in moves:
        out.wait()


def per_device(latent, timesteps, w_qkv, w_out, w_time, stale_kv):
    anywhere = pl.BlockSpec(memory_space=pl.ANY)
    dma = pltpu.SemaphoreType.DMA
    results = [
        jax.ShapeDtypeStruct((ROWS, WIDTH), BF16),
        jax.ShapeDtypeStruct((ROWS, WIDTH), BF16),
        jax.ShapeDtypeStruct((2, D, WIDTH), BF16),
    ]
    made = pl.pallas_call(
        kernel,
        out_shape=results,
        in_specs=[pl.BlockSpec(memory_space=pltpu.SMEM)] + [anywhere] * 5,
        out_specs=[anywhere] * 3,
        scratch_shapes=[
            pltpu.VMEM((ROWS, WIDTH), BF16),
            pltpu.VMEM((ROWS, WIDTH), BF16),
            pltpu.VMEM((ROWS, WIDTH), BF16),
            pltpu.VMEM((ROWS, WIDTH), F32),
            pltpu.VMEM((WIDTH, 2304), BF16),
            pltpu.VMEM((QW, WIDTH), BF16),
            pltpu.VMEM((FREQ, 3 * WIDTH), BF16),
            pltpu.VMEM((8, 3 * WIDTH), F32),
            pltpu.VMEM((6, 2, D, D), BF16),
            pltpu.VMEM((3, 4, 3, 2, D, D), BF16),
            pltpu.VMEM((2, 2, 16, D, D), BF16),
            pltpu.VMEM((2, 2, 3, 16, 2, 16, D), BF16),
            pltpu.VMEM((2, 8, D, D), BF16),
            pltpu.VMEM((2, 3, 8, 2, 16, D), BF16),
            pltpu.VMEM((2, 8, D + 16, D), BF16),
            pltpu.VMEM((2, 6, D + 16, D), BF16),
            pltpu.VMEM((2, 8, 112, D), BF16),
            pltpu.VMEM((2, 8, 112, D), BF16),
            pltpu.VMEM((2 * D, 16 * D), F32),
            pltpu.VMEM((8 * D, 16 * D), BF16),
            pltpu.VMEM((8 * D, 1), F32),
            pltpu.VMEM((6, D, D), F32),
            pltpu.VMEM((6, D, 1), F32),
            pltpu.VMEM((3, 2, D, D), F32),
            pltpu.VMEM((3, 2, D, 1), F32),
            pltpu.VMEM((ROWS, QW), BF16),
            dma((4,)), dma((12,)), dma((2, 6)), dma((12,)),
            dma((2, 2)), dma((2, 2)), dma((2,)), dma((2,)),
            dma((2,)), dma((2,)), dma((2,)), dma((2,)),
            dma((2,)), dma((2,)), dma((2,)), dma((2,)),
        ],
        compiler_params=pltpu.CompilerParams(
            collective_id=0, has_side_effects=True, vmem_limit_bytes=62 * 2**20),
        cost_estimate=pl.CostEstimate(
            flops=8_000_000_000, bytes_accessed=18_000_000, transcendentals=5_000_000),
    )(timesteps, latent.reshape(ROWS, WIDTH), stale_kv, w_qkv, w_out, w_time)
    x_out, vel, next_kv = pl.pallas_call(
        hand_on,
        out_shape=results,
        in_specs=[anywhere] * 3,
        out_specs=[anywhere] * 3,
        scratch_shapes=[pltpu.VMEM(one.shape, BF16) for one in results] + [dma((3,)), dma((3,))],
        compiler_params=pltpu.CompilerParams(vmem_limit_bytes=60 * 2**20),
    )(*made)
    shape = (2, D, WIDTH)
    return x_out.reshape(shape), vel.reshape(shape), next_kv


def solution(mesh):
    tokens = P("frame", "patch", None)
    return jax.shard_map(
        per_device,
        mesh=mesh,
        in_specs=(tokens, P(), P(), P(), P(), tokens),
        out_specs=(tokens, tokens, tokens),
        check_vma=False,
    )
```

```python
import functools
import math

import jax
import jax.numpy as jnp
from jax import lax
from jax.experimental import pallas as pl
from jax.experimental.pallas import tpu as pltpu
from jax.sharding import PartitionSpec as P

MESH = pl.DeviceIdType.MESH
D = 128
SH = 3
TH = 3
WIDTH = 1536
QW = (SH + TH) * D
ROWS = 256
FREQ = 256
STEPS = 2
NEG = -1e30
LOG2 = math.log2(math.e) / math.sqrt(D)
F32 = jnp.float32
BF16 = jnp.bfloat16


def dot_t(a, b):
    return lax.dot_general(a, b, (((1,), (1,)), ((), ())), preferred_element_type=F32)


def iota(shape, dim):
    return lax.broadcasted_iota(jnp.int32, shape, dim)


def split3(value):
    hi = value.astype(BF16).astype(F32)
    mid = (value - hi).astype(BF16).astype(F32)
    return hi, mid, value - hi - mid


def col_to_row(col):
    eye = iota((D, D), 0) == iota((D, D), 1)
    return jnp.sum(jnp.where(eye, col, 0.0), axis=0, keepdims=True)


def sigma_of(index):
    unit = index.astype(F32) / 1000.0
    return 5.0 * unit / (1.0 + 4.0 * unit)


def kernel(
    ts_ref, lat_ref, stale_ref, wqkv_ref, wout_ref, wtime_ref,
    xo_ref, vo_ref, kvo_ref,
    x_v, h_v, vel_v, part_v, wqkv_v, wout_v, wtime_v, mods_v,
    qloc, kvloc, kvs, kvt, qs, qt, oss, osr, ots, otr,
    s_v, p_v, inv_v, ol_s, ll_s, ol_t, ll_t, att,
    load_sem, stale_sem, out_sem, kvo_sem,
    ks_s, ks_r, kt_s, kt_r, qs_s, qs_r, qt_s, qt_r, os_s, os_r, ot_s, ot_r,
):
    fi = lax.axis_index("frame")
    pi = lax.axis_index("patch")
    core = lax.rem(fi, 2)
    zh = lax.rem(fi // 2, 2)
    own = (fi // 4) * 2 + core
    half = lax.rem(pi, 4) // 2
    src = (pi // 4) * 2 + lax.rem(pi, 2)
    role = lax.rem(src + 4 * core, 8)

    def patch_at(place, of_half):
        return (place // 2) * 4 + 2 * of_half + lax.rem(place, 2)

    def place_of(pair):
        return lax.rem(pair + 8 - 4 * core, 8)

    def frame_at(owner, group):
        return (owner // 2) * 4 + group * 2 + lax.rem(owner, 2)

    def push(source, target, send, recv, device, is_self):
        @pl.when(is_self)
        def _():
            pltpu.make_async_copy(source, target, recv).start()

        @pl.when(jnp.logical_not(is_self))
        def _():
            pltpu.make_async_remote_copy(
                src_ref=source, dst_ref=target, send_sem=send, recv_sem=recv,
                device_id=device, device_id_type=MESH,
            ).start()

    def take(ref, sem):
        pltpu.make_async_copy(ref, ref, sem).wait()

    def take_sent(all_of_them, but_one, sem):
        @pl.when(role < 6)
        def _():
            take(but_one, sem)

        @pl.when(role >= 6)
        def _():
            take(all_of_them, sem)

    def loop(count, body):
        def step(index, carry):
            body(index)
            return carry
        lax.fori_loop(0, count, step, 0)

    barrier = pltpu.get_barrier_semaphore()

    def greet(k):
        pl.semaphore_signal(
            barrier, inc=1, device_id=(fi, lax.rem(pi + k + 1, 16)), device_id_type=MESH)
        pl.semaphore_signal(
            barrier, inc=1, device_id=(lax.rem(fi + k + 1, 16), pi), device_id_type=MESH)

    loop(15, greet)

    def load_stale(block):
        return pltpu.make_async_copy(
            stale_ref.at[:, :, pl.ds(pl.multiple_of(block * D, D), D)],
            kvloc.at[0, block // 3, lax.rem(block, 3)], stale_sem.at[block])

    loop(12, lambda b: load_stale(b).start())
    loads = [
        pltpu.make_async_copy(a, b, load_sem.at[n])
        for n, (a, b) in enumerate(
            [(lat_ref, x_v), (wtime_ref, wtime_v), (wqkv_ref, wqkv_v), (wout_ref, wout_v)])
    ]
    for one in loads:
        one.start()

    loop(12, lambda b: load_stale(b).wait())
    pl.semaphore_wait(barrier, 30)

    def send_spatial(k, kv):
        def one(n):
            to_half = lax.rem(half + 1 + n // 6, 2)
            pair = lax.rem(n, 6)
            frame, head = pair // 3, lax.rem(pair, 3)
            device = patch_at(place_of(pair), to_half)
            slot = src + 8 * jnp.where(to_half == half, 0, 1)
            push(kvloc.at[k, kv, head, frame], kvs.at[k, kv, slot], ks_s.at[k, kv], ks_r.at[k, kv],
                 (fi, device), device == pi)

        loop(12, one)

    def send_temporal(k, first, count):
        def one(turn):
            n = first + turn
            group = lax.rem(zh + 1 + n, 2)
            owner = lax.rem(n // 2 + own, 8)
            device = frame_at(owner, group)
            slot = own + 8 * jnp.where(group == zh, 0, 1)
            rows = pl.ds(pl.multiple_of(owner * 16, 16), 16)
            push(kvloc.at[k, 2:4, :, :, rows], kvt.at[k, :, :, slot], kt_s.at[k], kt_r.at[k],
                 (device, pi), device == fi)

        loop(count, one)

    send_spatial(0, 0)

    loads[1].wait()
    lane = iota((16, D), 1).astype(F32)
    row = iota((16, D), 0)
    level = jnp.where(
        row < 3, sigma_of(jnp.full((16, D), ts_ref[0], jnp.int32)),
        sigma_of(jnp.full((16, D), ts_ref[1], jnp.int32))) * 1000.0
    angles = level * jnp.exp(-math.log(10000.0) * lane / D)
    part = lax.rem(row, 3)

    def embed(value):
        value = value / (1.0 + jnp.exp(-value))
        hi, mid, low = split3(value)
        return jnp.where(part == 0, hi, jnp.where(part == 1, mid, low)).astype(BF16)

    emb = jnp.concatenate([embed(jnp.cos(angles)), embed(jnp.sin(angles))], axis=1)
    for n in range(0, 3 * WIDTH, 512):
        cols = slice(n, n + 512)
        parts = jnp.dot(emb, wtime_v[:, cols], preferred_element_type=F32)
        for k in range(STEPS):
            mods_v[k : k + 1, cols] = jnp.sum(parts[3 * k : 3 * k + 3], axis=0, keepdims=True)

    loads[0].wait()

    def sent_queries(k):
        take_sent(qs.at[k, 0:6], qs.at[k, 0:5], qs_s.at[k])
        take(qt.at[k, :, 0:7], qt_s.at[k])

    for k in range(STEPS):
        def norm(n):
            rows = pl.ds(pl.multiple_of(n * 32, 32), 32)
            value = x_v[rows, :].astype(F32)
            center = jnp.mean(value, axis=-1, keepdims=True)
            value = value - center
            spread = jnp.mean(value * value, axis=-1, keepdims=True)
            value = value * lax.rsqrt(spread + 1e-06)
            h_v[rows, :] = (
                value * (1.0 + mods_v[k : k + 1, WIDTH : 2 * WIDTH]) + mods_v[k : k + 1, :WIDTH]
            ).astype(BF16)

        loop(ROWS // 32, norm)
        if k == 0:
            loads[2].wait()

        def project(n):
            cols = pl.ds(pl.multiple_of(n * 256, 256), 256)
            return jnp.dot(h_v[...], wqkv_v[:, cols], preferred_element_type=F32).astype(BF16)

        def query(n):
            out = project(n)
            for part_n in range(2):
                qloc[2 * n + part_n] = out[:, part_n * D : (part_n + 1) * D].reshape(2, D, D)

        if k > 0:
            sent_queries(k - 1)
        loop(3, query)

        def send_q(pair):
            place = place_of(pair)
            frame, head = pair // 3, lax.rem(pair, 3)
            push(qloc.at[head, frame], qs.at[k, src], qs_s.at[k], qs_r.at[k],
                 (fi, patch_at(place, half)), place == src)

        def send_qt(owner):
            rows = pl.ds(pl.multiple_of(owner * 16, 16), 16)
            push(qloc.at[3:6, :, rows], qt.at[k, :, own], qt_s.at[k], qt_r.at[k],
                 (frame_at(owner, zh), pi), owner == own)

        loop(6, send_q)
        loop(8, send_qt)
        if k == 0:
            send_spatial(0, 1)
            send_temporal(0, 0, 10)
        else:
            send_temporal(1, 8, 8)

        def fresh(n):
            out = project(n + 3)
            for part_n in range(2):
                block = 2 * n + part_n
                kvloc[k + 1, block // 3, lax.rem(block, 3)] = out[:, part_n * D : (part_n + 1) * D].reshape(2, D, D)

        loop(6, fresh)

        def store_kv(block):
            return pltpu.make_async_copy(
                kvloc.at[STEPS, block // 3, lax.rem(block, 3)],
                kvo_ref.at[:, :, pl.ds(pl.multiple_of(block * D, D), D)], kvo_sem.at[block])

        if k + 1 == STEPS:
            loop(12, lambda b: store_kv(b).start())

        def local_spatial(pair):
            frame, head = pair // 3, pair % 3
            scores = dot_t(qloc[head, frame], kvloc[k + 1, 0, head, frame]) * LOG2
            top = jnp.max(scores, axis=-1, keepdims=True)
            expo = jnp.exp2(scores - top)
            total = jnp.sum(expo, axis=-1, keepdims=True)
            out = jnp.dot(expo.astype(BF16), kvloc[k + 1, 1, head, frame], preferred_element_type=F32)
            ol_s[pair] = out / total
            ll_s[pair] = top + jnp.log2(total)

        for pair in range(6):
            local_spatial(pair)

        def local_temporal(head):
            for frame in range(2):
                q = qloc[3 + head, frame].astype(F32)
                s0, s1 = [
                    jnp.sum(q * kvloc[k + 1, 2, head, f].astype(F32), axis=-1, keepdims=True) * LOG2
                    for f in range(2)
                ]
                top = jnp.maximum(s0, s1)
                e0, e1 = jnp.exp2(s0 - top), jnp.exp2(s1 - top)
                total = e0 + e1
                out = e0 * kvloc[k + 1, 3, head, 0].astype(F32) + e1 * kvloc[k + 1, 3, head, 1].astype(F32)
                ol_t[head, frame] = out / total
                ll_t[head, frame] = top + jnp.log2(total)

        for head in range(TH):
            local_temporal(head)

        @pl.when(role < 6)
        def _():
            take(qs.at[k], qs_r.at[k])
            take(kvs.at[k, 0], ks_r.at[k, 0])

            def weigh(n):
                q = qs[k, pl.ds(2 * n, 2)].reshape(2 * D, D)
                s_v[...] = dot_t(q, kvs[k, 0].reshape(16 * D, D))
                base = pl.multiple_of(n * 2 * D, 2 * D)
                s_v[0:D, pl.ds(base, D)] = jnp.full((D, D), NEG, F32)
                s_v[D : 2 * D, pl.ds(pl.multiple_of(base + D, D), D)] = jnp.full((D, D), NEG, F32)
                scores = s_v[...]
                top = jnp.max(scores, axis=-1, keepdims=True)
                expo = jnp.exp2((scores - top) * LOG2)
                total = jnp.sum(expo, axis=-1, keepdims=True)
                p_v[pl.ds(base, 2 * D), :] = expo.astype(BF16)
                inv_v[pl.ds(base, 2 * D), :] = 1.0 / total
                lse = top * LOG2 + jnp.log2(total)
                for part_n in range(2):
                    hi, mid, low = split3(col_to_row(lse[part_n * D : (part_n + 1) * D]))
                    tile = iota((16, D), 0)
                    oss[k, 2 * n + part_n, D : D + 16] = jnp.where(
                        tile == 0, hi, jnp.where(tile == 1, mid, jnp.where(tile == 2, low, 0.0))).astype(BF16)

            loop(4, weigh)

        @pl.when(role < 6)
        def _():
            take(kvs.at[k, 1], ks_r.at[k, 1])

            def attend(turn):
                n = lax.rem(turn + role, 4)
                rows = pl.ds(pl.multiple_of(n * 2 * D, 2 * D), 2 * D)
                out = jnp.dot(p_v[rows, :], kvs[k, 1].reshape(16 * D, D), preferred_element_type=F32)
                out = (out * inv_v[rows, :]).astype(BF16)
                for part_n in range(2):
                    place = 2 * n + part_n
                    oss[k, place, 0:D] = out[part_n * D : (part_n + 1) * D]
                    push(oss.at[k, place], osr.at[k, role], os_s.at[k], os_r.at[k],
                         (fi, patch_at(place, half)), place == src)

            loop(4, attend)

        if k + 1 < STEPS:
            send_temporal(0, 10, 6)
            send_spatial(1, 0)
            send_spatial(1, 1)

        take(qt.at[k], qt_r.at[k])
        take(kvt.at[k], kt_r.at[k])
        rows_i, cols_i = iota((ROWS, 2 * ROWS), 0), iota((ROWS, 2 * ROWS), 1)
        seen = (lax.rem(rows_i, 16) == lax.rem(cols_i, 16)) & (rows_i // 32 != cols_i // 32)
        tile = iota((16, D), 0)
        stats = [jnp.zeros((16, D), F32), jnp.zeros((16, D), F32)]
        for head in range(TH):
            scores = dot_t(qt[k, head].reshape(ROWS, D), kvt[k, 0, head].reshape(2 * ROWS, D))
            scores = jnp.where(seen, scores, NEG)
            top = jnp.max(scores, axis=-1, keepdims=True)
            expo = jnp.exp2((scores - top) * LOG2)
            total = jnp.sum(expo, axis=-1, keepdims=True)
            out = jnp.dot(
                expo.astype(BF16), kvt[k, 1, head].reshape(2 * ROWS, D), preferred_element_type=F32)
            out = (out / total).astype(BF16)
            lse = top * LOG2 + jnp.log2(total)
            ots[k, :, head * 32 : head * 32 + 32] = out.reshape(8, 32, D)
            for chunk in range(2):
                parts = split3(col_to_row(lse[chunk * D : (chunk + 1) * D]))
                for n, value in enumerate(parts):
                    stats[chunk] = jnp.where(tile == 3 * head + n, value, stats[chunk])
        for place in range(8):
            ots[k, place, 96:112] = stats[place // 4].astype(BF16)

        def send_ot(place):
            push(ots.at[k, place], otr.at[k, own], ot_s.at[k], ot_r.at[k],
                 (frame_at(place, zh), pi), place == own)

        loop(8, send_ot)

        if k + 1 < STEPS:
            send_temporal(1, 0, 8)

        def merge(mine, mine_lse, other, other_lse):
            weight = 1.0 / (1.0 + jnp.exp2(mine_lse - other_lse))
            return (mine + weight * (other.astype(F32) - mine)).astype(BF16)

        def columns(pick, stat, at):
            lse = dot_t(pick.astype(BF16), stat)
            return [jnp.sum(lse[:, c : c + 3], axis=-1, keepdims=True) for c in at]

        take(osr.at[k], os_r.at[k])
        lse_s = columns(
            iota((D, D), 0) == iota((D, D), 1), osr[k, :, D : D + 16].reshape(6 * 16, D), [16 * p for p in range(6)])
        for pair in range(6):
            frame, head = pair // 3, pair % 3
            att[frame * D : (frame + 1) * D, head * D : (head + 1) * D] = merge(
                ol_s[pair], ll_s[pair], osr[k, pair, 0:D], lse_s[pair])

        if k == 0:
            loads[3].wait()

        def first_half(n):
            cols = pl.ds(pl.multiple_of(n * 256, 256), 256)
            part_v[:, cols] = jnp.dot(
                att[:, : SH * D], wout_v[: SH * D, cols], preferred_element_type=F32)

        loop(WIDTH // 256, first_half)

        take(otr.at[k], ot_r.at[k])
        pick = iota((32, D), 1) == iota((32, D), 0) + 32 * lax.rem(own, 4)
        lse_t = columns(
            pick, otr[k, :, 96:112].reshape(8 * 16, D), [16 * o + 3 * h for o in range(8) for h in range(TH)])
        for owner in range(8):
            for head in range(TH):
                for frame in range(2):
                    rows = slice(owner * 16, owner * 16 + 16)
                    att[frame * D + owner * 16 : frame * D + owner * 16 + 16, (SH + head) * D : (SH + head + 1) * D] = merge(
                        ol_t[head, frame, rows], ll_t[head, frame, rows],
                        otr[k, owner, head * 32 + frame * 16 : head * 32 + frame * 16 + 16],
                        lse_t[owner * TH + head][frame * 16 : frame * 16 + 16])

        dsig = (sigma_of(jnp.full((1, 256), ts_ref[k + 1], jnp.int32))
                - sigma_of(jnp.full((1, 256), ts_ref[k], jnp.int32)))

        def stores(n):
            cols = pl.ds(pl.multiple_of(n * 256, 256), 256)
            return [
                pltpu.make_async_copy(x_v.at[:, cols], xo_ref.at[:, cols], out_sem.at[0, n]),
                pltpu.make_async_copy(vel_v.at[:, cols], vo_ref.at[:, cols], out_sem.at[1, n]),
            ]

        def update(n):
            cols = pl.ds(pl.multiple_of(n * 256, 256), 256)
            branch = part_v[:, cols] + jnp.dot(
                att[:, SH * D :], wout_v[SH * D :, cols], preferred_element_type=F32)
            vel = mods_v[k : k + 1, pl.ds(pl.multiple_of(2 * WIDTH + n * 256, 256), 256)] * branch
            x_v[:, cols] = (x_v[:, cols].astype(F32) + dsig * vel).astype(BF16)
            if k + 1 == STEPS:
                vel_v[:, cols] = vel.astype(BF16)
                for one in stores(n):
                    one.start()

        loop(WIDTH // 256, update)

    for k in range(STEPS):
        for kv in range(2):
            take_sent(kvs.at[k, kv, 0:12], kvs.at[k, kv, 0:11], ks_s.at[k, kv])
        take(kvt.at[k, :, :, 0:15], kt_s.at[k])

        @pl.when(role < 6)
        def _():
            take(oss.at[k, 0:7], os_s.at[k])

        take(ots.at[k, 0:7], ot_s.at[k])
    sent_queries(STEPS - 1)
    loop(12, lambda b: store_kv(b).wait())

    def stored(n):
        for one in stores(n):
            one.wait()

    loop(WIDTH // 256, stored)


def hand_on(a_ref, b_ref, c_ref, ao_ref, bo_ref, co_ref, a_v, b_v, c_v, in_sem, out_sem):
    moves = [
        (pltpu.make_async_copy(a, v, in_sem.at[n]), pltpu.make_async_copy(v, b, out_sem.at[n]))
        for n, (a, v, b) in enumerate([(a_ref, a_v, ao_ref), (b_ref, b_v, bo_ref), (c_ref, c_v, co_ref)])
    ]
    for into, _ in moves:
        into.start()
    for into, out in moves:
        into.wait()
        out.start()
    for _, out in moves:
        out.wait()


def per_device(latent, timesteps, w_qkv, w_out, w_time, stale_kv):
    anywhere = pl.BlockSpec(memory_space=pl.ANY)
    dma = pltpu.SemaphoreType.DMA
    results = [
        jax.ShapeDtypeStruct((ROWS, WIDTH), BF16),
        jax.ShapeDtypeStruct((ROWS, WIDTH), BF16),
        jax.ShapeDtypeStruct((2, D, WIDTH), BF16),
    ]
    made = pl.pallas_call(
        kernel,
        out_shape=results,
        in_specs=[pl.BlockSpec(memory_space=pltpu.SMEM)] + [anywhere] * 5,
        out_specs=[anywhere] * 3,
        scratch_shapes=[
            pltpu.VMEM((ROWS, WIDTH), BF16),
            pltpu.VMEM((ROWS, WIDTH), BF16),
            pltpu.VMEM((ROWS, WIDTH), BF16),
            pltpu.VMEM((ROWS, WIDTH), F32),
            pltpu.VMEM((WIDTH, 2304), BF16),
            pltpu.VMEM((QW, WIDTH), BF16),
            pltpu.VMEM((FREQ, 3 * WIDTH), BF16),
            pltpu.VMEM((8, 3 * WIDTH), F32),
            pltpu.VMEM((6, 2, D, D), BF16),
            pltpu.VMEM((3, 4, 3, 2, D, D), BF16),
            pltpu.VMEM((2, 2, 16, D, D), BF16),
            pltpu.VMEM((2, 2, 3, 16, 2, 16, D), BF16),
            pltpu.VMEM((2, 8, D, D), BF16),
            pltpu.VMEM((2, 3, 8, 2, 16, D), BF16),
            pltpu.VMEM((2, 8, D + 16, D), BF16),
            pltpu.VMEM((2, 6, D + 16, D), BF16),
            pltpu.VMEM((2, 8, 112, D), BF16),
            pltpu.VMEM((2, 8, 112, D), BF16),
            pltpu.VMEM((2 * D, 16 * D), F32),
            pltpu.VMEM((8 * D, 16 * D), BF16),
            pltpu.VMEM((8 * D, 1), F32),
            pltpu.VMEM((6, D, D), F32),
            pltpu.VMEM((6, D, 1), F32),
            pltpu.VMEM((3, 2, D, D), F32),
            pltpu.VMEM((3, 2, D, 1), F32),
            pltpu.VMEM((ROWS, QW), BF16),
            dma((4,)), dma((12,)), dma((2, 6)), dma((12,)),
            dma((2, 2)), dma((2, 2)), dma((2,)), dma((2,)),
            dma((2,)), dma((2,)), dma((2,)), dma((2,)),
            dma((2,)), dma((2,)), dma((2,)), dma((2,)),
        ],
        compiler_params=pltpu.CompilerParams(
            collective_id=0, has_side_effects=True, vmem_limit_bytes=62 * 2**20),
        cost_estimate=pl.CostEstimate(
            flops=8_000_000_000, bytes_accessed=18_000_000, transcendentals=5_000_000),
    )(timesteps, latent.reshape(ROWS, WIDTH), stale_kv, w_qkv, w_out, w_time)
    x_out, vel, next_kv = pl.pallas_call(
        hand_on,
        out_shape=results,
        in_specs=[anywhere] * 3,
        out_specs=[anywhere] * 3,
        scratch_shapes=[pltpu.VMEM(one.shape, BF16) for one in results] + [dma((3,)), dma((3,))],
        compiler_params=pltpu.CompilerParams(vmem_limit_bytes=60 * 2**20),
    )(*made)
    shape = (2, D, WIDTH)
    return x_out.reshape(shape), vel.reshape(shape), next_kv


def solution(mesh):
    tokens = P("frame", "patch", None)
    return jax.shard_map(
        per_device,
        mesh=mesh,
        in_specs=(tokens, P(), P(), P(), P(), tokens),
        out_specs=(tokens, tokens, tokens),
        check_vma=False,
    )
```
